768 devices in a mesh: tm: 48 (over z_lo, y), wafer: 8 (over x, core), sim: 2 (over z_hi).
Axes of the slice: x: 4, y: 8, z: 12 (z_hi: 2, z_lo: 6; z = z_hi * 6 + z_lo), core: 2. Of those that a mesh axis runs over, the one named last changes fastest.
Arguments:
- sky: bfloat16 [64, 8, 384], P('sim', 'wafer'), may hold values from -6 to 6
- taps: bfloat16 [8, 2048], P('wafer', 'sim'), may hold values from -0.125 to 0.125
- weights: float32 [8], P('wafer'), may hold values from 0.01 to 0.06
- pixels: int32 [8, 98304], P('wafer', 'tm'), may hold values from 0 to 384
- tiles: int32 [8, 768], P('wafer', 'tm'), may hold values from 0 to 7
Outputs:
- binned_sky_maps: float32 [64, 8, 384], P('sim', 'wafer')
The draws below stay inside these ranges and needn't reach their ends.
Inputs may be any that keep to these rules, and one draw needn't show every extreme that they name: `pixels`: the value 384 marks a padded sample, which reads zero and is not binned.
All inputs are finite; a program needn't handle non-finite values.
Results may differ from the reference program's by a relative error of at most 0.0029.
Values may be sent and summed in bfloat16 or wider, within the bound.
A program may use at most 32 MiB of HBM per device.

```python
import math
import jax
import jax.numpy as jnp
from jax import lax

SKIES = 64
TAPS = 2048
TILE_PIXELS = 384
DETECTORS = 8
SAMPLES = 98304
TILES = 8


def plant(result, stream_key, low, largest):
    place = [jax.random.randint(jax.random.fold_in(stream_key, axis), (), 0, length) for axis, length in enumerate(result.shape)]
    main_axis = result.shape.index(max(result.shape))
    next_to = place[:main_axis] + [(place[main_axis] + 1) % result.shape[main_axis]] + place[main_axis + 1:]
    return result.at[tuple(place)].set(low).at[tuple(next_to)].set(largest)


def steps_of(stream_key, extent, pieces, smallest, top_value):
    def one(position, shards_of):
        heights = jax.random.uniform(jax.random.fold_in(jax.random.fold_in(stream_key, 6), position), (shards_of,), jnp.float32, smallest / len(pieces), top_value / len(pieces))
        return jnp.repeat(jnp.exp(heights), extent[position] // shards_of).reshape((-1,) + (1,) * (len(extent) - position - 1))

    gain = one(*pieces[0])
    for cut in pieces[1:]:
        gain = gain * one(*cut)
    return gain


def centred(own_key, dims, spread, reach, split=(), kind=jnp.bfloat16):
    array = jax.random.normal(own_key, dims, jnp.float32) * spread
    if len(split) > 0:
        array = steps_of(own_key, dims, split, -0.22, 0.18) * array
    return jnp.clip(array, min=-reach, max=reach).astype(kind)


def setup_inputs(seed: int = 0) -> dict:
    streams_of = jax.random.split(jax.random.key(seed), 6)
    sky = centred(streams_of[0], (SKIES, TILES, TILE_PIXELS), 1.0, 6.0, ((0, 2), (1, 8)))
    taps = centred(streams_of[1], (DETECTORS, TAPS), TAPS ** -0.5, 0.125, ((0, 8), (1, 2)))
    weights = jnp.clip(jnp.exp(math.log(0.06) - 1.7917595 * jax.random.uniform(streams_of[2], (DETECTORS,), jnp.float32) ** steps_of(streams_of[2], (DETECTORS,), ((0, 8),), -0.2, 0.2)), 0.01, 0.06)
    pixels = plant(jax.random.randint(streams_of[3], (DETECTORS, SAMPLES), 0, TILE_PIXELS + 1), jax.random.fold_in(streams_of[3], 1), 0, TILE_PIXELS).astype(jnp.int32)
    tiles = plant(jax.random.randint(streams_of[4], (DETECTORS, SAMPLES // 128), 0, TILES), jax.random.fold_in(streams_of[4], 1), 0, TILES - 1).astype(jnp.int32)
    return dict(sky=sky, taps=taps, weights=weights, pixels=pixels, tiles=tiles)


def band_blocks(tap_row, taps_len):
    count = taps_len // 128 + 1
    block_idx = jnp.arange(count, dtype=jnp.int32)[:, None, None]
    row_idx = jnp.arange(128, dtype=jnp.int32)[None, :, None]
    col_idx = jnp.arange(128, dtype=jnp.int32)[None, None, :]
    lag = 128 * block_idx + col_idx - row_idx
    inside = (lag >= 0) & (lag < taps_len)
    values = jnp.take(tap_row, jnp.clip(lag, 0, taps_len - 1).astype(jnp.int32))
    return jnp.where(inside, values, jnp.zeros_like(values))


def reference(sky, taps, weights, pixels, tiles):
    lead_blocks = TAPS // 128
    out_blocks = SAMPLES // 128
    flat_sky = sky.reshape(SKIES, TILES * TILE_PIXELS)

    def one_detector(running, item):
        pix_row, tile_row, tap_row, weight_one = item
        sample_tile = jnp.repeat(tile_row, 128)
        is_live = pix_row < TILE_PIXELS
        flat_index = (sample_tile * TILE_PIXELS + jnp.minimum(pix_row, TILE_PIXELS - 1)).astype(jnp.int32)
        picked = flat_sky[:, flat_index]
        stream = jnp.where(is_live[None, :], picked, jnp.zeros_like(picked)).astype(jnp.bfloat16)
        extended = jnp.concatenate([jnp.zeros((SKIES, TAPS), jnp.bfloat16), stream], axis=1)
        blocked = extended.reshape(SKIES, -1, 128).astype(jnp.float32)
        toeplitz_matrix = band_blocks(tap_row, TAPS).astype(jnp.float32)
        filtered_stream = jnp.zeros((SKIES, out_blocks, 128), jnp.float32)
        for start_offset in range(lead_blocks + 1):
            filter_window = blocked[:, lead_blocks - start_offset:lead_blocks - start_offset + out_blocks]
            filtered_stream = filtered_stream + jnp.einsum("xyl,le->xye", filter_window, toeplitz_matrix[start_offset])
        weighted = (weight_one * filtered_stream).astype(jnp.bfloat16).reshape(SKIES, SAMPLES)
        target = jnp.where(is_live, flat_index, TILES * TILE_PIXELS).astype(jnp.int32)
        binned = jax.ops.segment_sum(weighted.astype(jnp.float32).T, target, num_segments=TILES * TILE_PIXELS + 1)
        return running + binned[:TILES * TILE_PIXELS].T, None

    start = jnp.zeros((SKIES, TILES * TILE_PIXELS), jnp.float32)
    total, _ = lax.scan(one_detector, start, (pixels, tiles, taps, weights))
    return total.reshape(SKIES, TILES, TILE_PIXELS)
```

```python
import functools

import jax
import jax.numpy as jnp
from jax import lax
from jax.experimental import pallas as pl
from jax.experimental.pallas import tpu as pltpu
from jax.sharding import PartitionSpec as P

MESH = pl.DeviceIdType.MESH
Y = 8
CHUNK = 256


def kernel(
    dims,
    sky_ref,
    taps_ref,
    weights_ref,
    pixels_ref,
    tiles_ref,
    out_ref,
    sky_all,
    taps_all,
    code_ref,
    prev_ref,
    onehot_ref,
    toep_ref,
    stream_ref,
    part_ref,
    core_in,
    x_out,
    x_in,
    y_out,
    y_in,
    z_out,
    z_in,
    full_ref,
    sky_sem,
    tap_sem,
    code_sem,
    core_sem,
    x_sem,
    y_sem,
    z_sem,
    g_sem,
):
    tm_count, wafer_count = dims
    z_count = tm_count // Y
    x_count = wafer_count // 2
    skies, pixel_count = sky_ref.shape
    half = taps_ref.shape[1]
    taps_len = 2 * half
    time_here = pixels_ref.shape[1]
    chunks = time_here // CHUNK
    lead = taps_len // CHUNK
    tm = lax.axis_index("tm")
    wafer = lax.axis_index("wafer")
    sim = lax.axis_index("sim")
    y, z = tm % Y, tm // Y
    x, core = wafer // 2, wafer % 2

    wafers = [{"wafer": (wafer + k) % wafer_count} for k in range(1, wafer_count)]
    other_core = {"wafer": x * 2 + 1 - core}
    xs = [(x + k) % x_count for k in range(1, x_count)]
    ys = [(y + k) % Y for k in range(1, Y)]
    zs = [(z + k) % z_count for k in range(1, z_count)]
    y_ids = [{"tm": z * Y + k} for k in ys]
    z_ids = [{"tm": k * Y + y} for k in zs]
    other_sim = {"sim": 1 - sim}

    barrier = pltpu.get_barrier_semaphore()
    partners = wafers + y_ids + z_ids + [other_sim]
    for partner in partners:
        pl.semaphore_signal(barrier, inc=1, device_id=partner, device_id_type=MESH)

    @pl.when(tm > 0)
    def _():
        pl.semaphore_signal(barrier, inc=1, device_id={"tm": tm - 1}, device_id_type=MESH)

    for block in range(time_here // 128):
        lanes = slice(block * 128, block * 128 + 128)
        code_ref[:, lanes] = pixels_ref[:, lanes] + 512 * tiles_ref[0, block]

    pl.semaphore_wait(barrier, len(partners) + (tm < tm_count - 1).astype(jnp.int32))

    sends = []

    def send(source, target, sems, index, device):
        copy = pltpu.make_async_remote_copy(
            src_ref=source,
            dst_ref=target,
            send_sem=sems.at[0, index],
            recv_sem=sems.at[1, index],
            device_id=device,
            device_id_type=MESH,
        )
        copy.start()
        sends.append(copy)
        return copy

    code_copy = pltpu.make_async_remote_copy(
        src_ref=code_ref,
        dst_ref=prev_ref,
        send_sem=code_sem.at[0],
        recv_sem=code_sem.at[1],
        device_id={"tm": (tm + 1) % tm_count},
        device_id_type=MESH,
    )

    @pl.when(tm < tm_count - 1)
    def _():
        code_copy.start()

    tap_copy = send(taps_ref, taps_all.at[sim], tap_sem, 0, other_sim)
    sky_copies = [send(sky_ref, sky_all.at[wafer], sky_sem, k, d) for k, d in enumerate(wafers)]
    sky_all[wafer] = sky_ref[...]
    taps_all[sim] = taps_ref[...]

    pixel_id = lax.broadcasted_iota(jnp.int32, (pixel_count, CHUNK), 0)

    def indicator(code):
        return jnp.where(pixel_id == (code & 511), 1.0, 0.0).astype(jnp.bfloat16)

    for n in range(chunks):
        lanes = slice(n * CHUNK, (n + 1) * CHUNK)
        onehot_ref[:, lanes] = indicator(code_ref[:, lanes])

    tap_copy.wait_recv()
    edge = jnp.zeros((1, CHUNK), jnp.float32)
    row = jnp.concatenate(
        [edge, taps_all[0].astype(jnp.float32), taps_all[1].astype(jnp.float32), edge], axis=1
    )
    spread = jnp.broadcast_to(row, (128, row.shape[1]))
    toep_ref[...] = pltpu.roll(spread, 0, 1, stride=1, stride_axis=0).astype(jnp.bfloat16)

    for copy in sky_copies:
        copy.wait_recv()
    panels = sky_all[...].reshape(wafer_count * skies, pixel_count)

    def pick(table, code):
        dense = jnp.dot(panels, table, preferred_element_type=jnp.float32)
        tile = code >> 9
        picked = dense[:skies]
        for g in range(1, wafer_count):
            picked = jnp.where(tile == g, dense[g * skies : (g + 1) * skies], picked)
        return picked.astype(jnp.bfloat16)

    for n in range(chunks):
        lanes = slice(n * CHUNK, (n + 1) * CHUNK)
        stream_ref[(lead + n) * skies : (lead + n + 1) * skies] = pick(
            onehot_ref[:, lanes], code_ref[:, lanes]
        )

    @pl.when(tm > 0)
    def _():
        code_copy.wait_recv()
        for n in range(lead):
            lanes = slice(n * CHUNK, (n + 1) * CHUNK)
            code = prev_ref[:, lanes]
            stream_ref[n * skies : (n + 1) * skies] = pick(indicator(code), code)

    @pl.when(tm == 0)
    def _():
        stream_ref[: lead * skies] = jnp.zeros((lead * skies, CHUNK), jnp.bfloat16)

    rows = chunks * skies
    windows = jnp.concatenate([stream_ref[m * skies : m * skies + rows] for m in range(lead + 1)], axis=1)
    bands = []
    for m in range(lead + 1):
        at = taps_len + CHUNK - CHUNK * m
        bands += [toep_ref[:, at : at + CHUNK], toep_ref[:, at - 128 : at - 128 + CHUNK]]
    filtered = jnp.dot(windows, jnp.concatenate(bands, axis=0), preferred_element_type=jnp.float32)
    weighted = (weights_ref[0] * filtered).astype(jnp.bfloat16)

    order = [2 * i + c for c in range(2) for i in range(x_count)]
    zero = jnp.zeros((skies, CHUNK), jnp.bfloat16)
    columns = []
    for n in range(chunks):
        tile = code_ref[:, n * CHUNK : (n + 1) * CHUNK] >> 9
        piece = weighted[n * skies : (n + 1) * skies]
        columns.append(jnp.concatenate([jnp.where(tile == g, piece, zero) for g in order], axis=0))
    part = lax.dot_general(
        jnp.concatenate(columns, axis=1),
        onehot_ref[...],
        (((1,), (1,)), ((), ())),
        preferred_element_type=jnp.float32,
    )
    part_ref[...] = part.reshape(2, x_count, skies, pixel_count)

    send(part_ref.at[1 - core], core_in, core_sem, 0, other_core).wait_recv()
    x_out[...] = part_ref[core] + core_in[...]

    copies = [
        send(x_out.at[k], x_in.at[i], x_sem, i, {"wafer": 2 * k + core}) for i, k in enumerate(xs)
    ]
    for copy in copies:
        copy.wait_recv()
    total = x_out[x]
    for i in range(x_count - 1):
        total += x_in[i]
    share = skies // Y
    for k in range(Y):
        y_out[k] = total[k * share : (k + 1) * share]

    copies = [send(y_out.at[k], y_in.at[i], y_sem, i, d) for i, (k, d) in enumerate(zip(ys, y_ids))]
    for copy in copies:
        copy.wait_recv()
    total = y_out[y]
    for i in range(Y - 1):
        total += y_in[i]
    z_out[...] = total

    copies = [send(z_out, z_in.at[i], z_sem, i, d) for i, d in enumerate(z_ids)]
    for copy in copies:
        copy.wait_recv()
    z_in[z_count - 1] = total
    total = jnp.zeros_like(total)
    for k in range(z_count):
        total += z_in[(z - k + z_count - 1) % z_count]
    full_ref[y] = total

    copies = [send(full_ref.at[y], full_ref.at[y], g_sem, i, d) for i, d in enumerate(y_ids)]
    for copy in copies:
        copy.wait_recv()
    for k in range(Y):
        out_ref[k * share : (k + 1) * share] = full_ref[k]

    for copy in sends:
        copy.wait_send()

    @pl.when(tm < tm_count - 1)
    def _():
        code_copy.wait_send()


def solution(mesh):
    tm_count, wafer_count = mesh.shape["tm"], mesh.shape["wafer"]

    def per_device(sky, taps, weights, pixels, tiles):
        skies, _, pixel_count = sky.shape
        half, time_here = taps.shape[1], pixels.shape[1]
        lead, chunks = 2 * half // CHUNK, time_here // CHUNK
        x_count, z_count, share = wafer_count // 2, tm_count // Y, skies // Y
        vmem = pl.BlockSpec(memory_space=pltpu.VMEM)
        smem = pl.BlockSpec(memory_space=pltpu.SMEM)
        f32, bf16 = jnp.float32, jnp.bfloat16
        sems = lambda n: pltpu.SemaphoreType.DMA((2, n))
        maps = pl.pallas_call(
            functools.partial(kernel, (tm_count, wafer_count)),
            out_shape=jax.ShapeDtypeStruct((skies, pixel_count), f32),
            in_specs=[vmem, vmem, smem, vmem, smem],
            out_specs=vmem,
            scratch_shapes=[
                pltpu.VMEM((wafer_count, skies, pixel_count), bf16),
                pltpu.VMEM((2, 1, half), bf16),
                pltpu.VMEM((1, time_here), jnp.int32),
                pltpu.VMEM((1, time_here), jnp.int32),
                pltpu.VMEM((pixel_count, time_here), bf16),
                pltpu.VMEM((128, 2 * half + 2 * CHUNK), bf16),
                pltpu.VMEM(((lead + chunks) * skies, CHUNK), bf16),
                pltpu.VMEM((2, x_count, skies, pixel_count), f32),
                pltpu.VMEM((x_count, skies, pixel_count), f32),
                pltpu.VMEM((x_count, skies, pixel_count), f32),
                pltpu.VMEM((x_count - 1, skies, pixel_count), f32),
                pltpu.VMEM((Y, share, pixel_count), f32),
                pltpu.VMEM((Y - 1, share, pixel_count), f32),
                pltpu.VMEM((share, pixel_count), f32),
                pltpu.VMEM((z_count, share, pixel_count), f32),
                pltpu.VMEM((Y, share, pixel_count), f32),
                sems(wafer_count - 1),
                sems(1),
                pltpu.SemaphoreType.DMA((2,)),
                sems(1),
                sems(x_count - 1),
                sems(Y - 1),
                sems(z_count - 1),
                sems(Y - 1),
            ],
            compiler_params=pltpu.CompilerParams(
                collective_id=0, has_side_effects=True, vmem_limit_bytes=40 * 1024 * 1024
            ),
        )(sky.reshape(skies, pixel_count), taps, weights, pixels, tiles)
        return maps.reshape(skies, 1, pixel_count)

    placed = (
        P("sim", "wafer", None),
        P("wafer", "sim"),
        P("wafer"),
        P("wafer", "tm"),
        P("wafer", "tm"),
    )
    return jax.shard_map(
        per_device, mesh=mesh, in_specs=placed, out_specs=P("sim", "wafer", None), check_vma=False
    )
```

```python
import functools

import jax
import jax.numpy as jnp
from jax import lax
from jax.experimental import pallas as pl
from jax.experimental.pallas import tpu as pltpu
from jax.sharding import PartitionSpec as P

MESH = pl.DeviceIdType.MESH
Y = 8
CHUNK = 256
LANES = 128
Y_STEPS = (4, 3, 5, 2, 6, 1, 7)


def kernel(
    dims,
    sky_ref,
    taps_ref,
    weights_ref,
    pixels_ref,
    tiles_ref,
    out_ref,
    sky_all,
    sky_wide,
    table_ref,
    taps_all,
    weight_ref,
    pix_all,
    tile_in,
    tile_all,
    onehot_ref,
    toep_ref,
    stream_ref,
    part_ref,
    part_in,
    z_out,
    z_in,
    full_ref,
    local_sem,
    sky_sem,
    tap_sem,
    pix_sem,
    tile_sem,
    w_sem,
    z_sem,
    g_sem,
    z_ready,
    tap_ready,
):
    tm_count, wafer_count = dims
    z_count = tm_count // Y
    half_rows = sky_all.shape[1]
    share = table_ref.shape[1] // 2
    panels = sky_ref.shape[1] // LANES
    groups = panels
    half = taps_ref.shape[1]
    taps_len = 2 * half
    time_here = pixels_ref.shape[1]
    chunks = time_here // CHUNK
    lead = taps_len // CHUNK
    rows = Y * share
    tm = lax.axis_index("tm")
    wafer = lax.axis_index("wafer")
    sim = lax.axis_index("sim")
    y, z = tm % Y, tm // Y
    per_half = half_rows // share

    ws = [(wafer + k) % wafer_count for k in range(1, wafer_count)]
    ys = [(y + k) % Y for k in Y_STEPS]
    zs = [(z + k) % z_count for k in range(1, z_count)]
    w_ids = [{"wafer": k} for k in ws]
    y_ids = [{"tm": z * Y + k} for k in ys]
    z_ids = [{"tm": k * Y + y} for k in zs]

    gives_taps = z == 0
    gives_first = jnp.logical_and(gives_taps, sim == 1)
    gives_last = jnp.logical_and(gives_taps, sim == 0)
    tap_ids = [{"sim": 1 - sim, "tm": k * Y + y} for k in range(z_count)]
    tap_giver = {"sim": 1 - sim, "tm": y}
    gives_halo = jnp.logical_and(y == Y - 1, z < z_count - 1)
    halo_ids = [{"tm": (z + 1) % z_count * Y + k} for k in range(Y)]

    barrier = pltpu.get_barrier_semaphore()

    def greet(device, sem=barrier):
        pl.semaphore_signal(sem, inc=1, device_id=device, device_id_type=MESH)

    for partner in y_ids + w_ids:
        greet(partner)

    @pl.when(z > 0)
    def _():
        greet({"tm": (z - 1) * Y + Y - 1})

    @pl.when(sim == 0)
    def _():
        greet(tap_giver)

    @pl.when(gives_last)
    def _():
        for partner in tap_ids:
            greet(partner)

    for k in range(1, z_count):

        @pl.when(z + k < z_count)
        def _():
            greet({"tm": (z + k) * Y + y})

    sky_half = sky_ref.at[pl.ds(pl.multiple_of(y // per_half * half_rows, half_rows), half_rows)]
    locals_ = [
        pltpu.make_async_copy(sky_half, sky_all.at[wafer], local_sem.at[0]),
        pltpu.make_async_copy(taps_ref, taps_all.at[sim], local_sem.at[1]),
        pltpu.make_async_copy(weights_ref, weight_ref, local_sem.at[2]),
        pltpu.make_async_copy(pixels_ref, pix_all.at[y + 1], local_sem.at[3]),
        pltpu.make_async_copy(tiles_ref, tile_in.at[y + 1], local_sem.at[4]),
    ]
    for copy in locals_:
        copy.start()

    @pl.when(z == 0)
    def _():
        pix_all[0] = jnp.full((1, time_here), panels * LANES, jnp.int32)
        tile_in[0] = jnp.zeros((1, tile_in.shape[2]), jnp.int32)

    count = len(y_ids) + len(w_ids) + z
    count += jnp.where(gives_halo, Y, 0) + jnp.where(gives_first, z_count, 0) + jnp.where(sim == 1, 1, 0)
    pl.semaphore_wait(barrier, count)

    sends = []

    def remote(source, target, sems, index, device):
        return pltpu.make_async_remote_copy(
            src_ref=source,
            dst_ref=target,
            send_sem=sems.at[0, index],
            recv_sem=sems.at[1, index],
            device_id=device,
            device_id_type=MESH,
        )

    def send(*args):
        copy = remote(*args)
        copy.start()
        sends.append(copy)
        return copy

    def wait_all(copies):
        for copy in copies:
            copy.wait_recv()

    def give(source, target, sems, base, devices):
        return [
            pltpu.make_async_remote_copy(
                src_ref=source,
                dst_ref=target,
                send_sem=sems.at[0, base + i],
                recv_sem=sems.at[1, base],
                device_id=d,
                device_id_type=MESH,
            )
            for i, d in enumerate(devices)
        ]

    pix_copies = [send(pixels_ref, pix_all.at[y + 1], pix_sem, i, d) for i, d in enumerate(y_ids)]
    tile_copies = [send(tiles_ref, tile_in.at[y + 1], tile_sem, i, d) for i, d in enumerate(y_ids)]
    halo_tiles = give(tiles_ref, tile_in.at[0], tile_sem, Y - 1, halo_ids)
    halo_pixels = give(pixels_ref, pix_all.at[0], pix_sem, Y - 1, halo_ids)
    tap_copies = give(taps_ref, taps_all.at[sim], tap_sem, 0, tap_ids)

    @pl.when(gives_halo)
    def _():
        for copy in halo_tiles + halo_pixels:
            copy.start()

    @pl.when(gives_first)
    def _():
        for copy in tap_copies:
            copy.start()

    for k in range(1, z_count):

        @pl.when(z >= k)
        def _():
            greet({"tm": (z - k) * Y + y}, z_ready)

    @pl.when(sim == 1)
    def _():
        greet(tap_giver, tap_ready)

    sky_copies = [send(sky_half, sky_all.at[wafer], sky_sem, i, d) for i, d in enumerate(w_ids)]
    for copy in locals_:
        copy.wait()

    wait_all(sky_copies)
    for g in range(wafer_count):
        wide = sky_all[g].astype(jnp.float32)
        for k in range(per_half):
            sky_wide[g, k] = wide[k * share : (k + 1) * share]
    for g in range(wafer_count):
        mine = sky_wide[g, y % per_half]
        table_ref[g] = jnp.concatenate([mine, mine], axis=0)

    def spread_taps():
        tap_copies[0].wait_recv()
        edge = jnp.zeros((1, CHUNK), jnp.float32)
        row = jnp.concatenate(
            [edge, taps_all[0].astype(jnp.float32), taps_all[1].astype(jnp.float32), edge], axis=1
        )
        spread = jnp.broadcast_to(row, (LANES, row.shape[1]))
        toep_ref[...] = pltpu.roll(spread, 0, 1, stride=1, stride_axis=0).astype(jnp.bfloat16)

    taps_first = z >= z_count // 2
    pl.when(taps_first)(spread_taps)

    wait_all(tile_copies)

    @pl.when(z > 0)
    def _():
        halo_tiles[0].wait_recv()

    to_scalar = pltpu.make_async_copy(tile_in, tile_all, local_sem.at[0])
    to_scalar.start()

    lane_id = lax.broadcasted_iota(jnp.int32, (LANES, CHUNK), 0)
    def lower(pix):
        return jnp.where(pix < panels * LANES, pix & (LANES - 1), -1)

    def indicate(k):
        for n in range(chunks):
            lanes = slice(n * CHUNK, (n + 1) * CHUNK)
            low = lower(pix_all[k + 1, :, lanes])
            onehot_ref[k, :, lanes] = jnp.where(lane_id == low, 1.0, 0.0).astype(jnp.bfloat16)

    indicate(y)
    for i in reversed(range(Y - 1)):
        pix_copies[i].wait_recv()
        indicate((y + Y - Y_STEPS[i]) % Y)

    @pl.when(z > 0)
    def _():
        halo_pixels[0].wait_recv()

    to_scalar.wait()

    upper = lax.broadcasted_iota(jnp.int32, (2 * share, LANES), 0) < share

    def pick(first, block):
        lanes = slice(block * LANES, (block + 1) * LANES)
        pix = jnp.where(upper, pix_all[first, :, lanes], pix_all[first + 1, :, lanes])
        table = jnp.where(
            jnp.concatenate([upper] * panels, axis=1),
            table_ref[tile_all[first, 0, block]],
            table_ref[tile_all[first + 1, 0, block]],
        )
        low, high = pix & (LANES - 1), pix >> 7
        found = jnp.zeros((2 * share, LANES), jnp.float32)
        for j in range(panels):
            part = jnp.take_along_axis(table[:, j * LANES : (j + 1) * LANES], low, axis=1)
            found = jnp.where(high == j, part, found)
        return found

    for n in range(chunks):
        early, late = [], []
        for h in range(CHUNK // LANES):
            block = n * (CHUNK // LANES) + h
            found = [pick(2 * p + 1, block) for p in range(Y // 2)]
            turned = [pltpu.roll(f, share, 0) for f in found]
            before = [pick(0, block)]
            before += [jnp.where(upper, turned[p - 1], turned[p]) for p in range(1, Y // 2)]
            early.append(jnp.concatenate(before, axis=0))
            late.append(jnp.concatenate(found, axis=0))
        for at, halves in ((n, early), (lead + n, late)):
            stream_ref[at * rows : (at + 1) * rows] = jnp.concatenate(halves, axis=1).astype(jnp.bfloat16)

    @pl.when(gives_last)
    def _():
        pl.semaphore_wait(tap_ready, z_count)
        for copy in tap_copies:
            copy.start()

    pl.when(jnp.logical_not(taps_first))(spread_taps)

    windows = jnp.concatenate(
        [stream_ref[m * rows : (m + chunks) * rows] for m in range(lead + 1)], axis=1
    )
    bands = []
    for m in range(lead + 1):
        at = taps_len + CHUNK - CHUNK * m
        bands += [toep_ref[:, at : at + CHUNK], toep_ref[:, at - LANES : at - LANES + CHUNK]]
    filtered = jnp.dot(windows, jnp.concatenate(bands, axis=0), preferred_element_type=jnp.float32)
    weighted = (weight_ref[0, 0] * filtered).astype(jnp.bfloat16).astype(jnp.float32)

    first_group = lax.broadcasted_iota(jnp.int32, (2 * share, LANES), 0) // share
    part = jnp.zeros((wafer_count * groups * share, LANES), jnp.float32)
    for k in range(Y):
        columns = []
        for n in range(chunks):
            for h in range(CHUNK // LANES):
                block = 2 * n + h
                at = n * rows + k // 2 * 2 * share
                both = weighted[at : at + 2 * share, h * LANES : (h + 1) * LANES]
                swapped = pltpu.roll(both, share, 0)
                mine = jnp.where(upper, both, swapped) if k % 2 == 0 else jnp.where(upper, swapped, both)
                group = (pix_all[k + 1, :, block * LANES : (block + 1) * LANES] >> 7) + (
                    groups * tile_all[k + 1, 0, block]
                )
                offset = group - first_group
                columns.append(
                    jnp.concatenate(
                        [jnp.where(offset == 2 * j, mine, 0.0) for j in range(wafer_count * groups // 2)],
                        axis=0,
                    ).astype(jnp.bfloat16)
                )
        part += lax.dot_general(
            jnp.concatenate(columns, axis=1),
            onehot_ref[k],
            (((1,), (1,)), ((), ())),
            preferred_element_type=jnp.float32,
        )
    for k in range(wafer_count * groups):
        part_ref[k // groups, k % groups] = part[k * share : (k + 1) * share]

    copies = [send(part_ref.at[k], part_in.at[i], w_sem, i, d) for i, (k, d) in enumerate(zip(ws, w_ids))]
    wait_all(copies)
    total = part_ref[wafer]
    for i in range(wafer_count - 1):
        total += part_in[i]
    z_out[...] = total

    @pl.when(z < z_count - 1)
    def _():
        pl.semaphore_wait(z_ready, z_count - 1 - z)

    wait_all([send(z_out, z_in.at[i], z_sem, i, d) for i, d in enumerate(z_ids)])
    z_in[z_count - 1] = total
    total = jnp.zeros_like(total)
    for k in range(z_count):
        total += z_in[(z - k + z_count - 1) % z_count]
    full_ref[y] = total

    wait_all([send(full_ref.at[y], full_ref.at[y], g_sem, i, d) for i, d in enumerate(y_ids)])
    for k in range(Y):
        for j in range(panels):
            out_ref[k * share : (k + 1) * share, j * LANES : (j + 1) * LANES] = full_ref[k, j]

    for copy in sends:
        copy.wait_send()

    @pl.when(gives_halo)
    def _():
        for copy in halo_tiles + halo_pixels:
            copy.wait_send()

    @pl.when(gives_taps)
    def _():
        for copy in tap_copies:
            copy.wait_send()


def solution(mesh):
    tm_count, wafer_count = mesh.shape["tm"], mesh.shape["wafer"]

    def per_device(sky, taps, weights, pixels, tiles):
        skies, _, pixel_count = sky.shape
        half, time_here, blocks = taps.shape[1], pixels.shape[1], tiles.shape[1]
        lead, chunks = 2 * half // CHUNK, time_here // CHUNK
        z_count, share = tm_count // Y, skies // Y
        hbm = pl.BlockSpec(memory_space=pltpu.HBM)
        f32, bf16, i32 = jnp.float32, jnp.bfloat16, jnp.int32
        piece = (pixel_count // LANES, share, LANES)
        sems = lambda n: pltpu.SemaphoreType.DMA((2, n))
        maps = pl.pallas_call(
            functools.partial(kernel, (tm_count, wafer_count)),
            out_shape=jax.ShapeDtypeStruct((skies, pixel_count), f32),
            in_specs=[hbm] * 5,
            out_specs=pl.BlockSpec(memory_space=pltpu.VMEM),
            scratch_shapes=[
                pltpu.VMEM((wafer_count, 16, pixel_count), bf16),
                pltpu.VMEM((wafer_count, 16 // share, share, pixel_count), f32),
                pltpu.VMEM((wafer_count, 2 * share, pixel_count), f32),
                pltpu.VMEM((2, 1, half), bf16),
                pltpu.SMEM((1, 1), f32),
                pltpu.VMEM((Y + 1, 1, time_here), i32),
                pltpu.VMEM((Y + 1, 1, blocks), i32),
                pltpu.SMEM((Y + 1, 1, blocks), i32),
                pltpu.VMEM((Y, LANES, time_here), bf16),
                pltpu.VMEM((LANES, 2 * half + 2 * CHUNK), bf16),
                pltpu.VMEM(((lead + chunks) * skies, CHUNK), bf16),
                pltpu.VMEM((wafer_count,) + piece, f32),
                pltpu.VMEM((wafer_count - 1,) + piece, f32),
                pltpu.VMEM(piece, f32),
                pltpu.VMEM((z_count,) + piece, f32),
                pltpu.VMEM((Y,) + piece, f32),
                pltpu.SemaphoreType.DMA((5,)),
                sems(wafer_count - 1),
                sems(z_count),
                sems(2 * Y - 1),
                sems(2 * Y - 1),
                sems(wafer_count - 1),
                sems(z_count - 1),
                sems(Y - 1),
                pltpu.SemaphoreType.REGULAR,
                pltpu.SemaphoreType.REGULAR,
            ],
            compiler_params=pltpu.CompilerParams(
                collective_id=0, has_side_effects=True, vmem_limit_bytes=60 * 1024 * 1024
            ),
        )(sky.reshape(skies, pixel_count), taps, weights.reshape(1, 1), pixels, tiles)
        return maps.reshape(skies, 1, pixel_count)

    placed = (
        P("sim", "wafer", None),
        P("wafer", "sim"),
        P("wafer"),
        P("wafer", "tm"),
        P("wafer", "tm"),
    )
    return jax.shard_map(
        per_device, mesh=mesh, in_specs=placed, out_specs=P("sim", "wafer", None), check_vma=False
    )
```

```python
import functools

import jax
import jax.numpy as jnp
from jax import lax
from jax.experimental import pallas as pl
from jax.experimental.pallas import tpu as pltpu
from jax.sharding import PartitionSpec as P

MESH = pl.DeviceIdType.MESH
Y = 8
CHUNK = 256
LANES = 128
Y_STEPS = (4, 3, 5, 2, 6, 1, 7)


def kernel(
    dims,
    sky_ref,
    taps_ref,
    weights_ref,
    pixels_ref,
    tiles_ref,
    out_ref,
    sky_all,
    sky_wide,
    table_ref,
    taps_all,
    weight_ref,
    pix_all,
    tile_in,
    tile_all,
    onehot_ref,
    toep_ref,
    stream_ref,
    part_ref,
    part_in,
    z_out,
    z_in,
    sum_ref,
    local_sem,
    sky_sem,
    tap_sem,
    pix_sem,
    tile_sem,
    w_sem,
    z_sem,
    g_sem,
    z_ready,
    tap_ready,
):
    tm_count, wafer_count = dims
    z_count = tm_count // Y
    half_rows = sky_all.shape[1]
    share = table_ref.shape[1] // 2
    panels = sky_ref.shape[1] // LANES
    groups = panels
    half = taps_ref.shape[1]
    taps_len = 2 * half
    time_here = pixels_ref.shape[1]
    chunks = time_here // CHUNK
    lead = taps_len // CHUNK
    rows = Y * share
    tm = lax.axis_index("tm")
    wafer = lax.axis_index("wafer")
    sim = lax.axis_index("sim")
    y, z = tm % Y, tm // Y
    per_half = half_rows // share

    ws = [(wafer + k) % wafer_count for k in range(1, wafer_count)]
    ys = [(y + k) % Y for k in Y_STEPS]
    zs = [(z + k) % z_count for k in range(1, z_count)]
    w_ids = [{"wafer": k} for k in ws]
    y_ids = [{"tm": z * Y + k} for k in ys]
    z_ids = [{"tm": k * Y + y} for k in zs]

    gives_taps = z == 0
    gives_first = jnp.logical_and(gives_taps, sim == 1)
    gives_last = jnp.logical_and(gives_taps, sim == 0)
    tap_ids = [{"sim": 1 - sim, "tm": k * Y + y} for k in range(z_count)]
    tap_giver = {"sim": 1 - sim, "tm": y}
    gives_halo = jnp.logical_and(y == Y - 1, z < z_count - 1)
    halo_ids = [{"tm": (z + 1) % z_count * Y + k} for k in range(Y)]

    barrier = pltpu.get_barrier_semaphore()

    def greet(device, sem=barrier):
        pl.semaphore_signal(sem, inc=1, device_id=device, device_id_type=MESH)

    for partner in y_ids + w_ids:
        greet(partner)

    @pl.when(z > 0)
    def _():
        greet({"tm": (z - 1) * Y + Y - 1})

    @pl.when(sim == 0)
    def _():
        greet(tap_giver)

    @pl.when(gives_last)
    def _():
        for partner in tap_ids:
            greet(partner)

    for k in range(1, z_count):

        @pl.when(z + k < z_count)
        def _():
            greet({"tm": (z + k) * Y + y})

    sky_half = sky_ref.at[pl.ds(pl.multiple_of(y // per_half * half_rows, half_rows), half_rows)]
    locals_ = [
        pltpu.make_async_copy(sky_half, sky_all.at[wafer], local_sem.at[0]),
        pltpu.make_async_copy(taps_ref, taps_all.at[sim], local_sem.at[1]),
        pltpu.make_async_copy(weights_ref, weight_ref, local_sem.at[2]),
        pltpu.make_async_copy(pixels_ref, pix_all.at[y + 1], local_sem.at[3]),
        pltpu.make_async_copy(tiles_ref, tile_in.at[y + 1], local_sem.at[4]),
    ]
    for copy in locals_:
        copy.start()

    @pl.when(z == 0)
    def _():
        pix_all[0] = jnp.full((1, time_here), panels * LANES, jnp.int32)
        tile_in[0] = jnp.zeros((1, tile_in.shape[2]), jnp.int32)

    count = len(y_ids) + len(w_ids) + z
    count += jnp.where(gives_halo, Y, 0) + jnp.where(gives_first, z_count, 0) + jnp.where(sim == 1, 1, 0)
    pl.semaphore_wait(barrier, count)

    sends = []

    def remote(source, target, sems, index, device):
        return pltpu.make_async_remote_copy(
            src_ref=source,
            dst_ref=target,
            send_sem=sems.at[0, index],
            recv_sem=sems.at[1, index],
            device_id=device,
            device_id_type=MESH,
        )

    def send(*args):
        copy = remote(*args)
        copy.start()
        sends.append(copy)
        return copy

    def wait_all(copies):
        for copy in copies:
            copy.wait_recv()

    def give(source, target, sems, base, devices):
        return [
            pltpu.make_async_remote_copy(
                src_ref=source,
                dst_ref=target,
                send_sem=sems.at[0, base + i],
                recv_sem=sems.at[1, base],
                device_id=d,
                device_id_type=MESH,
            )
            for i, d in enumerate(devices)
        ]

    tile_copies = [send(tiles_ref, tile_in.at[y + 1], tile_sem, i, d) for i, d in enumerate(y_ids)]
    pix_copies = [send(pixels_ref, pix_all.at[y + 1], pix_sem, i, d) for i, d in enumerate(y_ids)]
    halo_tiles = give(tiles_ref, tile_in.at[0], tile_sem, Y - 1, halo_ids)
    halo_pixels = give(pixels_ref, pix_all.at[0], pix_sem, Y - 1, halo_ids)
    tap_copies = give(taps_ref, taps_all.at[sim], tap_sem, 0, tap_ids)

    @pl.when(gives_halo)
    def _():
        for copy in halo_tiles + halo_pixels:
            copy.start()

    @pl.when(gives_first)
    def _():
        for copy in tap_copies:
            copy.start()

    for k in range(1, z_count):

        @pl.when(z >= k)
        def _():
            greet({"tm": (z - k) * Y + y}, z_ready)

    @pl.when(sim == 1)
    def _():
        greet(tap_giver, tap_ready)

    sky_copies = [send(sky_half, sky_all.at[wafer], sky_sem, i, d) for i, d in enumerate(w_ids)]
    for copy in locals_:
        copy.wait()

    wait_all(sky_copies)
    for g in range(wafer_count):
        wide = sky_all[g].astype(jnp.float32)
        for k in range(per_half):
            sky_wide[g, k] = wide[k * share : (k + 1) * share]
    for g in range(wafer_count):
        mine = sky_wide[g, y % per_half]
        table_ref[g] = jnp.concatenate([mine, mine], axis=0)

    def spread_taps():
        tap_copies[0].wait_recv()
        edge = jnp.zeros((1, CHUNK), jnp.float32)
        row = jnp.concatenate(
            [edge, taps_all[0].astype(jnp.float32), taps_all[1].astype(jnp.float32), edge], axis=1
        )
        spread = jnp.broadcast_to(row, (LANES, row.shape[1]))
        toep_ref[...] = pltpu.roll(spread, 0, 1, stride=1, stride_axis=0).astype(jnp.bfloat16)

    taps_first = z >= z_count // 2
    pl.when(taps_first)(spread_taps)

    wait_all(tile_copies)

    @pl.when(z > 0)
    def _():
        halo_tiles[0].wait_recv()

    to_scalar = pltpu.make_async_copy(tile_in, tile_all, local_sem.at[0])
    to_scalar.start()

    lane_id = lax.broadcasted_iota(jnp.int32, (LANES, CHUNK), 0)
    def lower(pix):
        return jnp.where(pix < panels * LANES, pix & (LANES - 1), -1)

    def indicate(k):
        for n in range(chunks):
            lanes = slice(n * CHUNK, (n + 1) * CHUNK)
            low = lower(pix_all[k + 1, :, lanes])
            onehot_ref[k, :, lanes] = jnp.where(lane_id == low, 1.0, 0.0).astype(jnp.bfloat16)

    indicate(y)
    for i in reversed(range(Y - 1)):
        pix_copies[i].wait_recv()
        indicate((y + Y - Y_STEPS[i]) % Y)

    @pl.when(z > 0)
    def _():
        halo_pixels[0].wait_recv()

    to_scalar.wait()

    upper = lax.broadcasted_iota(jnp.int32, (2 * share, LANES), 0) < share

    def pick(first, block):
        lanes = slice(block * LANES, (block + 1) * LANES)
        pix = jnp.where(upper, pix_all[first, :, lanes], pix_all[first + 1, :, lanes])
        table = jnp.where(
            jnp.concatenate([upper] * panels, axis=1),
            table_ref[tile_all[first, 0, block]],
            table_ref[tile_all[first + 1, 0, block]],
        )
        low, high = pix & (LANES - 1), pix >> 7
        found = jnp.zeros((2 * share, LANES), jnp.float32)
        for j in range(panels):
            part = jnp.take_along_axis(table[:, j * LANES : (j + 1) * LANES], low, axis=1)
            found = jnp.where(high == j, part, found)
        return found

    for n in range(chunks):
        early, late = [], []
        for h in range(CHUNK // LANES):
            block = n * (CHUNK // LANES) + h
            found = [pick(2 * p + 1, block) for p in range(Y // 2)]
            turned = [pltpu.roll(f, share, 0) for f in found]
            before = [pick(0, block)]
            before += [jnp.where(upper, turned[p - 1], turned[p]) for p in range(1, Y // 2)]
            early.append(jnp.concatenate(before, axis=0))
            late.append(jnp.concatenate(found, axis=0))
        for at, halves in ((n, early), (lead + n, late)):
            stream_ref[at * rows : (at + 1) * rows] = jnp.concatenate(halves, axis=1).astype(jnp.bfloat16)

    @pl.when(gives_last)
    def _():
        pl.semaphore_wait(tap_ready, z_count)
        for copy in tap_copies:
            copy.start()

    pl.when(jnp.logical_not(taps_first))(spread_taps)

    windows = jnp.concatenate(
        [stream_ref[m * rows : (m + chunks) * rows] for m in range(lead + 1)], axis=1
    )
    bands = []
    for m in range(lead + 1):
        at = taps_len + CHUNK - CHUNK * m
        bands += [toep_ref[:, at : at + CHUNK], toep_ref[:, at - LANES : at - LANES + CHUNK]]
    filtered = jnp.dot(windows, jnp.concatenate(bands, axis=0), preferred_element_type=jnp.float32)
    weighted = (weight_ref[0, 0] * filtered).astype(jnp.bfloat16).astype(jnp.float32)

    first_group = lax.broadcasted_iota(jnp.int32, (2 * share, LANES), 0) // share
    part = jnp.zeros((wafer_count * groups * share, LANES), jnp.float32)
    for k in range(Y):
        columns = []
        for n in range(chunks):
            for h in range(CHUNK // LANES):
                block = 2 * n + h
                at = n * rows + k // 2 * 2 * share
                both = weighted[at : at + 2 * share, h * LANES : (h + 1) * LANES]
                swapped = pltpu.roll(both, share, 0)
                mine = jnp.where(upper, both, swapped) if k % 2 == 0 else jnp.where(upper, swapped, both)
                group = (pix_all[k + 1, :, block * LANES : (block + 1) * LANES] >> 7) + (
                    groups * tile_all[k + 1, 0, block]
                )
                offset = group - first_group
                columns.append(
                    jnp.concatenate(
                        [jnp.where(offset == 2 * j, mine, 0.0) for j in range(wafer_count * groups // 2)],
                        axis=0,
                    ).astype(jnp.bfloat16)
                )
        part += lax.dot_general(
            jnp.concatenate(columns, axis=1),
            onehot_ref[k],
            (((1,), (1,)), ((), ())),
            preferred_element_type=jnp.float32,
        )
    for k in range(wafer_count):
        for j in range(groups):
            for sky in range(share):
                at, to = (k * groups + j) * share + sky, sky * groups + j
                part_ref[k, to // share, to % share : to % share + 1] = part[at : at + 1]

    copies = [send(part_ref.at[k], part_in.at[i], w_sem, i, d) for i, (k, d) in enumerate(zip(ws, w_ids))]
    wait_all(copies)
    total = part_ref[wafer]
    for i in range(wafer_count - 1):
        total += part_in[i]
    z_out[...] = total

    @pl.when(z < z_count - 1)
    def _():
        pl.semaphore_wait(z_ready, z_count - 1 - z)

    wait_all([send(z_out, z_in.at[i], z_sem, i, d) for i, d in enumerate(z_ids)])
    z_in[z_count - 1] = total
    total = jnp.zeros_like(total)
    for k in range(z_count):
        total += z_in[(z - k + z_count - 1) % z_count]
    sum_ref[...] = total

    copies = [send(sum_ref, out_ref.at[y], g_sem, i, d) for i, d in enumerate(y_ids)]
    own = pltpu.make_async_copy(sum_ref, out_ref.at[y], local_sem.at[1])
    own.start()
    own.wait()
    wait_all(copies)

    for copy in sends:
        copy.wait_send()

    @pl.when(gives_halo)
    def _():
        for copy in halo_tiles + halo_pixels:
            copy.wait_send()

    @pl.when(gives_taps)
    def _():
        for copy in tap_copies:
            copy.wait_send()


def solution(mesh):
    tm_count, wafer_count = mesh.shape["tm"], mesh.shape["wafer"]

    def per_device(sky, taps, weights, pixels, tiles):
        skies, _, pixel_count = sky.shape
        half, time_here, blocks = taps.shape[1], pixels.shape[1], tiles.shape[1]
        lead, chunks = 2 * half // CHUNK, time_here // CHUNK
        z_count, share = tm_count // Y, skies // Y
        hbm = pl.BlockSpec(memory_space=pltpu.HBM)
        f32, bf16, i32 = jnp.float32, jnp.bfloat16, jnp.int32
        piece = (pixel_count // LANES, share, LANES)
        sems = lambda n: pltpu.SemaphoreType.DMA((2, n))
        maps = pl.pallas_call(
            functools.partial(kernel, (tm_count, wafer_count)),
            out_shape=jax.ShapeDtypeStruct((Y,) + piece, f32),
            in_specs=[hbm] * 5,
            out_specs=hbm,
            scratch_shapes=[
                pltpu.VMEM((wafer_count, 16, pixel_count), bf16),
                pltpu.VMEM((wafer_count, 16 // share, share, pixel_count), f32),
                pltpu.VMEM((wafer_count, 2 * share, pixel_count), f32),
                pltpu.VMEM((2, 1, half), bf16),
                pltpu.SMEM((1, 1), f32),
                pltpu.VMEM((Y + 1, 1, time_here), i32),
                pltpu.VMEM((Y + 1, 1, blocks), i32),
                pltpu.SMEM((Y + 1, 1, blocks), i32),
                pltpu.VMEM((Y, LANES, time_here), bf16),
                pltpu.VMEM((LANES, 2 * half + 2 * CHUNK), bf16),
                pltpu.VMEM(((lead + chunks) * skies, CHUNK), bf16),
                pltpu.VMEM((wafer_count,) + piece, f32),
                pltpu.VMEM((wafer_count - 1,) + piece, f32),
                pltpu.VMEM(piece, f32),
                pltpu.VMEM((z_count,) + piece, f32),
                pltpu.VMEM(piece, f32),
                pltpu.SemaphoreType.DMA((5,)),
                sems(wafer_count - 1),
                sems(z_count),
                sems(2 * Y - 1),
                sems(2 * Y - 1),
                sems(wafer_count - 1),
                sems(z_count - 1),
                sems(Y - 1),
                pltpu.SemaphoreType.REGULAR,
                pltpu.SemaphoreType.REGULAR,
            ],
            compiler_params=pltpu.CompilerParams(
                collective_id=0, has_side_effects=True, vmem_limit_bytes=60 * 1024 * 1024
            ),
        )(sky.reshape(skies, pixel_count), taps, weights.reshape(1, 1), pixels, tiles)
        return maps.reshape(skies, 1, pixel_count)

    placed = (
        P("sim", "wafer", None),
        P("wafer", "sim"),
        P("wafer"),
        P("wafer", "tm"),
        P("wafer", "tm"),
    )
    return jax.shard_map(
        per_device, mesh=mesh, in_specs=placed, out_specs=P("sim", "wafer", None), check_vma=False
    )
```

```python
import functools

import jax
import jax.numpy as jnp
from jax import lax
from jax.experimental import pallas as pl
from jax.experimental.pallas import tpu as pltpu
from jax.sharding import PartitionSpec as P

MESH = pl.DeviceIdType.MESH
Y = 8
CHUNK = 256
LANES = 128
Y_STEPS = (4, 3, 5, 2, 6, 1, 7)


def kernel(
    dims,
    sky_ref,
    taps_ref,
    weights_ref,
    pixels_ref,
    tiles_ref,
    out_ref,
    sky_all,
    sky_wide,
    table_ref,
    taps_all,
    weight_ref,
    pix_all,
    tile_in,
    tile_all,
    onehot_ref,
    toep_ref,
    stream_ref,
    part_ref,
    part_in,
    z_out,
    z_in,
    sum_ref,
    local_sem,
    sky_sem,
    tap_sem,
    pix_sem,
    tile_sem,
    w_sem,
    z_sem,
    g_sem,
    z_ready,
    tap_ready,
):
    tm_count, wafer_count = dims
    z_count = tm_count // Y
    half_rows = sky_all.shape[1]
    share = table_ref.shape[1] // 2
    panels = sky_ref.shape[1] // LANES
    groups = panels
    half = taps_ref.shape[1]
    taps_len = 2 * half
    time_here = pixels_ref.shape[1]
    chunks = time_here // CHUNK
    lead = taps_len // CHUNK
    rows = Y * share
    tm = lax.axis_index("tm")
    wafer = lax.axis_index("wafer")
    sim = lax.axis_index("sim")
    y, z = tm % Y, tm // Y
    per_half = half_rows // share

    ws = [(wafer + k) % wafer_count for k in (4, 5, 3, 2, 6, 1, 7)]
    ys = [(y + k) % Y for k in Y_STEPS]
    zs = [(z + k) % z_count for k in range(1, z_count)]
    w_ids = [{"wafer": k} for k in ws]
    y_ids = [{"tm": z * Y + k} for k in ys]
    z_ids = [{"tm": k * Y + y} for k in zs]

    gives_taps = z == 0
    gives_first = jnp.logical_and(gives_taps, sim == 1)
    gives_last = jnp.logical_and(gives_taps, sim == 0)
    tap_ids = [{"sim": 1 - sim, "tm": k * Y + y} for k in range(z_count)]
    tap_giver = {"sim": 1 - sim, "tm": y}
    gives_halo = jnp.logical_and(y == Y - 1, z < z_count - 1)
    halo_ids = [{"tm": (z + 1) % z_count * Y + k} for k in range(Y)]

    barrier = pltpu.get_barrier_semaphore()

    def greet(device, sem=barrier):
        pl.semaphore_signal(sem, inc=1, device_id=device, device_id_type=MESH)

    for partner in y_ids + w_ids:
        greet(partner)

    @pl.when(z > 0)
    def _():
        greet({"tm": (z - 1) * Y + Y - 1})

    @pl.when(sim == 0)
    def _():
        greet(tap_giver)

    @pl.when(gives_last)
    def _():
        for partner in tap_ids:
            greet(partner)

    for k in range(1, z_count):

        @pl.when(z + k < z_count)
        def _():
            greet({"tm": (z + k) * Y + y})

    sky_half = sky_ref.at[pl.ds(pl.multiple_of(y // per_half * half_rows, half_rows), half_rows)]
    locals_ = [
        pltpu.make_async_copy(sky_half, sky_all.at[wafer], local_sem.at[0]),
        pltpu.make_async_copy(taps_ref, taps_all.at[sim], local_sem.at[1]),
        pltpu.make_async_copy(weights_ref, weight_ref, local_sem.at[2]),
        pltpu.make_async_copy(pixels_ref, pix_all.at[y + 1], local_sem.at[3]),
        pltpu.make_async_copy(tiles_ref, tile_in.at[y + 1], local_sem.at[4]),
    ]
    for copy in locals_:
        copy.start()

    @pl.when(z == 0)
    def _():
        pix_all[0] = jnp.full((1, time_here), panels * LANES, jnp.int32)
        tile_in[0] = jnp.zeros((1, tile_in.shape[2]), jnp.int32)

    count = len(y_ids) + len(w_ids) + z
    count += jnp.where(gives_halo, Y, 0) + jnp.where(gives_first, z_count, 0) + jnp.where(sim == 1, 1, 0)
    pl.semaphore_wait(barrier, count)

    sends = []

    def remote(source, target, sems, index, device):
        return pltpu.make_async_remote_copy(
            src_ref=source,
            dst_ref=target,
            send_sem=sems.at[0, index],
            recv_sem=sems.at[1, index],
            device_id=device,
            device_id_type=MESH,
        )

    def send(*args):
        copy = remote(*args)
        copy.start()
        sends.append(copy)
        return copy

    def wait_all(copies):
        for copy in copies:
            copy.wait_recv()

    def give(source, target, sems, base, devices):
        return [
            pltpu.make_async_remote_copy(
                src_ref=source,
                dst_ref=target,
                send_sem=sems.at[0, base + i],
                recv_sem=sems.at[1, base],
                device_id=d,
                device_id_type=MESH,
            )
            for i, d in enumerate(devices)
        ]

    tile_copies = [send(tiles_ref, tile_in.at[y + 1], tile_sem, i, d) for i, d in enumerate(y_ids)]
    pix_copies = [send(pixels_ref, pix_all.at[y + 1], pix_sem, i, d) for i, d in enumerate(y_ids)]
    halo_tiles = give(tiles_ref, tile_in.at[0], tile_sem, Y - 1, halo_ids)
    halo_pixels = give(pixels_ref, pix_all.at[0], pix_sem, Y - 1, halo_ids)
    tap_copies = give(taps_ref, taps_all.at[sim], tap_sem, 0, tap_ids)

    @pl.when(gives_halo)
    def _():
        for copy in halo_tiles + halo_pixels:
            copy.start()

    @pl.when(gives_first)
    def _():
        for copy in tap_copies:
            copy.start()

    for k in range(1, z_count):

        @pl.when(z >= k)
        def _():
            greet({"tm": (z - k) * Y + y}, z_ready)

    @pl.when(sim == 1)
    def _():
        greet(tap_giver, tap_ready)

    sky_copies = [send(sky_half, sky_all.at[wafer], sky_sem, i, d) for i, d in enumerate(w_ids)]
    for copy in locals_:
        copy.wait()

    wait_all(sky_copies)
    for g in range(wafer_count):
        wide = sky_all[g].astype(jnp.float32)
        for k in range(per_half):
            sky_wide[g, k] = wide[k * share : (k + 1) * share]
    for g in range(wafer_count):
        mine = sky_wide[g, y % per_half]
        table_ref[g] = jnp.concatenate([mine, mine], axis=0)

    def spread_taps():
        tap_copies[0].wait_recv()
        edge = jnp.zeros((1, CHUNK), jnp.float32)
        row = jnp.concatenate(
            [edge, taps_all[0].astype(jnp.float32), taps_all[1].astype(jnp.float32), edge], axis=1
        )
        spread = jnp.broadcast_to(row, (LANES, row.shape[1]))
        toep_ref[...] = pltpu.roll(spread, 0, 1, stride=1, stride_axis=0).astype(jnp.bfloat16)

    taps_first = z >= z_count // 2
    pl.when(taps_first)(spread_taps)

    wait_all(tile_copies)

    @pl.when(z > 0)
    def _():
        halo_tiles[0].wait_recv()

    to_scalar = pltpu.make_async_copy(tile_in, tile_all, local_sem.at[0])
    to_scalar.start()

    lane_id = lax.broadcasted_iota(jnp.int32, (LANES, CHUNK), 0)
    def lower(pix):
        return jnp.where(pix < panels * LANES, pix & (LANES - 1), -1)

    def indicate(k):
        for n in range(chunks):
            lanes = slice(n * CHUNK, (n + 1) * CHUNK)
            low = lower(pix_all[k + 1, :, lanes])
            onehot_ref[k, :, lanes] = jnp.where(lane_id == low, 1.0, 0.0).astype(jnp.bfloat16)

    indicate(y)
    for i in reversed(range(Y - 1)):
        pix_copies[i].wait_recv()
        indicate((y + Y - Y_STEPS[i]) % Y)

    @pl.when(z > 0)
    def _():
        halo_pixels[0].wait_recv()

    to_scalar.wait()

    upper = lax.broadcasted_iota(jnp.int32, (2 * share, LANES), 0) < share

    def pick(first, block):
        lanes = slice(block * LANES, (block + 1) * LANES)
        pix = jnp.where(upper, pix_all[first, :, lanes], pix_all[first + 1, :, lanes])
        table = jnp.where(
            jnp.concatenate([upper] * panels, axis=1),
            table_ref[tile_all[first, 0, block]],
            table_ref[tile_all[first + 1, 0, block]],
        )
        low, high = pix & (LANES - 1), pix >> 7
        found = jnp.zeros((2 * share, LANES), jnp.float32)
        for j in range(panels):
            part = jnp.take_along_axis(table[:, j * LANES : (j + 1) * LANES], low, axis=1)
            found = jnp.where(high == j, part, found)
        return found

    for n in range(chunks):
        early, late = [], []
        for h in range(CHUNK // LANES):
            block = n * (CHUNK // LANES) + h
            found = [pick(2 * p + 1, block) for p in range(Y // 2)]
            turned = [pltpu.roll(f, share, 0) for f in found]
            before = [pick(0, block)]
            before += [jnp.where(upper, turned[p - 1], turned[p]) for p in range(1, Y // 2)]
            early.append(jnp.concatenate(before, axis=0))
            late.append(jnp.concatenate(found, axis=0))
        for at, halves in ((n, early), (lead + n, late)):
            stream_ref[at * rows : (at + 1) * rows] = jnp.concatenate(halves, axis=1).astype(jnp.bfloat16)

    @pl.when(gives_last)
    def _():
        pl.semaphore_wait(tap_ready, z_count)
        for copy in tap_copies:
            copy.start()

    pl.when(jnp.logical_not(taps_first))(spread_taps)

    windows = jnp.concatenate(
        [stream_ref[m * rows : (m + chunks) * rows] for m in range(lead + 1)], axis=1
    )
    bands = []
    for m in range(lead + 1):
        at = taps_len + CHUNK - CHUNK * m
        bands += [toep_ref[:, at : at + CHUNK], toep_ref[:, at - LANES : at - LANES + CHUNK]]
    filtered = jnp.dot(windows, jnp.concatenate(bands, axis=0), preferred_element_type=jnp.float32)
    weighted = (weight_ref[0, 0] * filtered).astype(jnp.bfloat16).astype(jnp.float32)

    first_group = lax.broadcasted_iota(jnp.int32, (2 * share, LANES), 0) // share
    part = jnp.zeros((wafer_count * groups * share, LANES), jnp.float32)
    for k in range(Y):
        columns = []
        for n in range(chunks):
            for h in range(CHUNK // LANES):
                block = 2 * n + h
                at = n * rows + k // 2 * 2 * share
                both = weighted[at : at + 2 * share, h * LANES : (h + 1) * LANES]
                swapped = pltpu.roll(both, share, 0)
                mine = jnp.where(upper, both, swapped) if k % 2 == 0 else jnp.where(upper, swapped, both)
                group = (pix_all[k + 1, :, block * LANES : (block + 1) * LANES] >> 7) + (
                    groups * tile_all[k + 1, 0, block]
                )
                offset = group - first_group
                columns.append(
                    jnp.concatenate(
                        [jnp.where(offset == 2 * j, mine, 0.0) for j in range(wafer_count * groups // 2)],
                        axis=0,
                    ).astype(jnp.bfloat16)
                )
        part += lax.dot_general(
            jnp.concatenate(columns, axis=1),
            onehot_ref[k],
            (((1,), (1,)), ((), ())),
            preferred_element_type=jnp.float32,
        )
    for k in range(wafer_count):
        for j in range(groups):
            for sky in range(share):
                at, to = (k * groups + j) * share + sky, sky * groups + j
                part_ref[k, to // share, to % share : to % share + 1] = part[at : at + 1]

    copies = [send(part_ref.at[k], part_in.at[i], w_sem, i, d) for i, (k, d) in enumerate(zip(ws, w_ids))]
    total = part_ref[wafer]
    for i in reversed(range(wafer_count - 1)):
        copies[i].wait_recv()
        total += part_in[i]
    z_out[...] = total

    @pl.when(z < z_count - 1)
    def _():
        pl.semaphore_wait(z_ready, z_count - 1 - z)

    wait_all([send(z_out, z_in.at[i], z_sem, i, d) for i, d in enumerate(z_ids)])
    z_in[z_count - 1] = total
    total = jnp.zeros_like(total)
    for k in range(z_count):
        total += z_in[(z - k + z_count - 1) % z_count]
    sum_ref[...] = total

    copies = [send(sum_ref, out_ref.at[y], g_sem, i, d) for i, d in enumerate(y_ids)]
    own = pltpu.make_async_copy(sum_ref, out_ref.at[y], local_sem.at[1])
    own.start()
    own.wait()
    wait_all(copies)

    for copy in sends:
        copy.wait_send()

    @pl.when(gives_halo)
    def _():
        for copy in halo_tiles + halo_pixels:
            copy.wait_send()

    @pl.when(gives_taps)
    def _():
        for copy in tap_copies:
            copy.wait_send()


def solution(mesh):
    tm_count, wafer_count = mesh.shape["tm"], mesh.shape["wafer"]

    def per_device(sky, taps, weights, pixels, tiles):
        skies, _, pixel_count = sky.shape
        half, time_here, blocks = taps.shape[1], pixels.shape[1], tiles.shape[1]
        lead, chunks = 2 * half // CHUNK, time_here // CHUNK
        z_count, share = tm_count // Y, skies // Y
        hbm = pl.BlockSpec(memory_space=pltpu.HBM)
        f32, bf16, i32 = jnp.float32, jnp.bfloat16, jnp.int32
        piece = (pixel_count // LANES, share, LANES)
        sems = lambda n: pltpu.SemaphoreType.DMA((2, n))
        maps = pl.pallas_call(
            functools.partial(kernel, (tm_count, wafer_count)),
            out_shape=jax.ShapeDtypeStruct((Y,) + piece, f32),
            in_specs=[hbm] * 5,
            out_specs=hbm,
            scratch_shapes=[
                pltpu.VMEM((wafer_count, 16, pixel_count), bf16),
                pltpu.VMEM((wafer_count, 16 // share, share, pixel_count), f32),
                pltpu.VMEM((wafer_count, 2 * share, pixel_count), f32),
                pltpu.VMEM((2, 1, half), bf16),
                pltpu.SMEM((1, 1), f32),
                pltpu.VMEM((Y + 1, 1, time_here), i32),
                pltpu.VMEM((Y + 1, 1, blocks), i32),
                pltpu.SMEM((Y + 1, 1, blocks), i32),
                pltpu.VMEM((Y, LANES, time_here), bf16),
                pltpu.VMEM((LANES, 2 * half + 2 * CHUNK), bf16),
                pltpu.VMEM(((lead + chunks) * skies, CHUNK), bf16),
                pltpu.VMEM((wafer_count,) + piece, f32),
                pltpu.VMEM((wafer_count - 1,) + piece, f32),
                pltpu.VMEM(piece, f32),
                pltpu.VMEM((z_count,) + piece, f32),
                pltpu.VMEM(piece, f32),
                pltpu.SemaphoreType.DMA((5,)),
                sems(wafer_count - 1),
                sems(z_count),
                sems(2 * Y - 1),
                sems(2 * Y - 1),
                sems(wafer_count - 1),
                sems(z_count - 1),
                sems(Y - 1),
                pltpu.SemaphoreType.REGULAR,
                pltpu.SemaphoreType.REGULAR,
            ],
            compiler_params=pltpu.CompilerParams(
                collective_id=0, has_side_effects=True, vmem_limit_bytes=60 * 1024 * 1024
            ),
        )(sky.reshape(skies, pixel_count), taps, weights.reshape(1, 1), pixels, tiles)
        return maps.reshape(skies, 1, pixel_count)

    placed = (
        P("sim", "wafer", None),
        P("wafer", "sim"),
        P("wafer"),
        P("wafer", "tm"),
        P("wafer", "tm"),
    )
    return jax.shard_map(
        per_device, mesh=mesh, in_specs=placed, out_specs=P("sim", "wafer", None), check_vma=False
    )
```

```python
import functools

import jax
import jax.numpy as jnp
from jax import lax
from jax.experimental import pallas as pl
from jax.experimental.pallas import tpu as pltpu
from jax.sharding import PartitionSpec as P

MESH = pl.DeviceIdType.MESH
Y = 8
CHUNK = 256
LANES = 128
Y_STEPS = (4, 3, 5, 2, 6, 1, 7)


def kernel(
    dims,
    sky_ref,
    taps_ref,
    weights_ref,
    pixels_ref,
    tiles_ref,
    out_ref,
    sky_all,
    sky_wide,
    table_ref,
    taps_all,
    weight_ref,
    pix_all,
    tile_in,
    tile_all,
    onehot_ref,
    toep_ref,
    stream_ref,
    part_ref,
    part_in,
    z_out,
    z_in,
    sum_ref,
    local_sem,
    sky_sem,
    tap_sem,
    pix_sem,
    tile_sem,
    w_sem,
    z_sem,
    g_sem,
    z_ready,
    tap_ready,
):
    tm_count, wafer_count = dims
    z_count = tm_count // Y
    half_rows = sky_all.shape[1]
    share = table_ref.shape[1] // 2
    panels = sky_ref.shape[1] // LANES
    groups = panels
    half = taps_ref.shape[1]
    taps_len = 2 * half
    time_here = pixels_ref.shape[1]
    chunks = time_here // CHUNK
    lead = taps_len // CHUNK
    rows = Y * share
    tm = lax.axis_index("tm")
    wafer = lax.axis_index("wafer")
    sim = lax.axis_index("sim")
    y, z = tm % Y, tm // Y
    per_half = half_rows // share

    ws = [(wafer + k) % wafer_count for k in range(1, wafer_count)]
    ys = [(y + k) % Y for k in Y_STEPS]
    zs = [(z + k) % z_count for k in range(1, z_count)]
    w_ids = [{"wafer": k} for k in ws]
    y_ids = [{"tm": z * Y + k} for k in ys]
    z_ids = [{"tm": k * Y + y} for k in zs]

    gives_taps = z == 0
    gives_first = jnp.logical_and(gives_taps, sim == 1)
    gives_last = jnp.logical_and(gives_taps, sim == 0)
    tap_ids = [{"sim": 1 - sim, "tm": k * Y + y} for k in range(z_count)]
    tap_giver = {"sim": 1 - sim, "tm": y}
    gives_halo = jnp.logical_and(y == Y - 1, z < z_count - 1)
    halo_ids = [{"tm": (z + 1) % z_count * Y + k} for k in range(Y)]

    barrier = pltpu.get_barrier_semaphore()

    def greet(device, sem=barrier):
        pl.semaphore_signal(sem, inc=1, device_id=device, device_id_type=MESH)

    for partner in y_ids + w_ids:
        greet(partner)

    @pl.when(z > 0)
    def _():
        greet({"tm": (z - 1) * Y + Y - 1})

    @pl.when(sim == 0)
    def _():
        greet(tap_giver)

    @pl.when(gives_last)
    def _():
        for partner in tap_ids:
            greet(partner)

    for k in range(1, z_count):

        @pl.when(z + k < z_count)
        def _():
            greet({"tm": (z + k) * Y + y})

    sky_half = sky_ref.at[pl.ds(pl.multiple_of(y // per_half * half_rows, half_rows), half_rows)]
    locals_ = [
        pltpu.make_async_copy(sky_half, sky_all.at[wafer], local_sem.at[0]),
        pltpu.make_async_copy(taps_ref, taps_all.at[sim], local_sem.at[1]),
        pltpu.make_async_copy(weights_ref, weight_ref, local_sem.at[2]),
        pltpu.make_async_copy(pixels_ref, pix_all.at[y + 1], local_sem.at[3]),
        pltpu.make_async_copy(tiles_ref, tile_in.at[y + 1], local_sem.at[4]),
    ]
    for copy in locals_:
        copy.start()

    @pl.when(z == 0)
    def _():
        pix_all[0] = jnp.full((1, time_here), panels * LANES, jnp.int32)
        tile_in[0] = jnp.zeros((1, tile_in.shape[2]), jnp.int32)

    count = len(y_ids) + len(w_ids) + z
    count += jnp.where(gives_halo, Y, 0) + jnp.where(gives_first, z_count, 0) + jnp.where(sim == 1, 1, 0)
    pl.semaphore_wait(barrier, count)

    sends = []

    def remote(source, target, sems, index, device):
        return pltpu.make_async_remote_copy(
            src_ref=source,
            dst_ref=target,
            send_sem=sems.at[0, index],
            recv_sem=sems.at[1, index],
            device_id=device,
            device_id_type=MESH,
        )

    def send(*args):
        copy = remote(*args)
        copy.start()
        sends.append(copy)
        return copy

    def wait_all(copies):
        for copy in copies:
            copy.wait_recv()

    def give(source, target, sems, base, devices):
        return [
            pltpu.make_async_remote_copy(
                src_ref=source,
                dst_ref=target,
                send_sem=sems.at[0, base + i],
                recv_sem=sems.at[1, base],
                device_id=d,
                device_id_type=MESH,
            )
            for i, d in enumerate(devices)
        ]

    tile_copies, pix_copies = [], []
    for i, d in enumerate(y_ids):
        tile_copies.append(send(tiles_ref, tile_in.at[y + 1], tile_sem, i, d))
        pix_copies.append(send(pixels_ref, pix_all.at[y + 1], pix_sem, i, d))
    halo_tiles = give(tiles_ref, tile_in.at[0], tile_sem, Y - 1, halo_ids)
    halo_pixels = give(pixels_ref, pix_all.at[0], pix_sem, Y - 1, halo_ids)
    tap_copies = give(taps_ref, taps_all.at[sim], tap_sem, 0, tap_ids)

    @pl.when(gives_halo)
    def _():
        for copy in halo_tiles + halo_pixels:
            copy.start()

    @pl.when(gives_first)
    def _():
        for copy in tap_copies:
            copy.start()

    for k in range(1, z_count):

        @pl.when(z >= k)
        def _():
            greet({"tm": (z - k) * Y + y}, z_ready)

    @pl.when(sim == 1)
    def _():
        greet(tap_giver, tap_ready)

    sky_copies = [send(sky_half, sky_all.at[wafer], sky_sem, i, d) for i, d in enumerate(w_ids)]
    for copy in locals_:
        copy.wait()

    wait_all(sky_copies)
    for g in range(wafer_count):
        wide = sky_all[g].astype(jnp.float32)
        for k in range(per_half):
            sky_wide[g, k] = wide[k * share : (k + 1) * share]
    for g in range(wafer_count):
        mine = sky_wide[g, y % per_half]
        table_ref[g] = jnp.concatenate([mine, mine], axis=0)

    def spread_taps():
        tap_copies[0].wait_recv()
        edge = jnp.zeros((1, CHUNK), jnp.float32)
        row = jnp.concatenate(
            [edge, taps_all[0].astype(jnp.float32), taps_all[1].astype(jnp.float32), edge], axis=1
        )
        spread = jnp.broadcast_to(row, (LANES, row.shape[1]))
        toep_ref[...] = pltpu.roll(spread, 0, 1, stride=1, stride_axis=0).astype(jnp.bfloat16)

    taps_first = z >= z_count // 2
    pl.when(taps_first)(spread_taps)

    wait_all(tile_copies)

    @pl.when(z > 0)
    def _():
        halo_tiles[0].wait_recv()

    to_scalar = pltpu.make_async_copy(tile_in, tile_all, local_sem.at[0])
    to_scalar.start()

    lane_id = lax.broadcasted_iota(jnp.int32, (LANES, CHUNK), 0)
    def lower(pix):
        return jnp.where(pix < panels * LANES, pix & (LANES - 1), -1)

    def indicate(k):
        for n in range(chunks):
            lanes = slice(n * CHUNK, (n + 1) * CHUNK)
            low = lower(pix_all[k + 1, :, lanes])
            onehot_ref[k, :, lanes] = jnp.where(lane_id == low, 1.0, 0.0).astype(jnp.bfloat16)

    indicate(y)
    for i in reversed(range(Y - 1)):
        pix_copies[i].wait_recv()
        indicate((y + Y - Y_STEPS[i]) % Y)

    @pl.when(z > 0)
    def _():
        halo_pixels[0].wait_recv()

    to_scalar.wait()

    upper = lax.broadcasted_iota(jnp.int32, (2 * share, LANES), 0) < share

    def pick(first, block):
        lanes = slice(block * LANES, (block + 1) * LANES)
        pix = jnp.where(upper, pix_all[first, :, lanes], pix_all[first + 1, :, lanes])
        table = jnp.where(
            jnp.concatenate([upper] * panels, axis=1),
            table_ref[tile_all[first, 0, block]],
            table_ref[tile_all[first + 1, 0, block]],
        )
        low, high = pix & (LANES - 1), pix >> 7
        found = jnp.zeros((2 * share, LANES), jnp.float32)
        for j in range(panels):
            part = jnp.take_along_axis(table[:, j * LANES : (j + 1) * LANES], low, axis=1)
            found = jnp.where(high == j, part, found)
        return found

    for n in range(chunks):
        early, late = [], []
        for h in range(CHUNK // LANES):
            block = n * (CHUNK // LANES) + h
            found = [pick(2 * p + 1, block) for p in range(Y // 2)]
            turned = [pltpu.roll(f, share, 0) for f in found]
            before = [pick(0, block)]
            before += [jnp.where(upper, turned[p - 1], turned[p]) for p in range(1, Y // 2)]
            early.append(jnp.concatenate(before, axis=0))
            late.append(jnp.concatenate(found, axis=0))
        for at, halves in ((n, early), (lead + n, late)):
            stream_ref[at * rows : (at + 1) * rows] = jnp.concatenate(halves, axis=1).astype(jnp.bfloat16)

    @pl.when(gives_last)
    def _():
        pl.semaphore_wait(tap_ready, z_count)
        for copy in tap_copies:
            copy.start()

    pl.when(jnp.logical_not(taps_first))(spread_taps)

    windows = jnp.concatenate(
        [stream_ref[m * rows : (m + chunks) * rows] for m in range(lead + 1)], axis=1
    )
    bands = []
    for m in range(lead + 1):
        at = taps_len + CHUNK - CHUNK * m
        bands += [toep_ref[:, at : at + CHUNK], toep_ref[:, at - LANES : at - LANES + CHUNK]]
    filtered = jnp.dot(windows, jnp.concatenate(bands, axis=0), preferred_element_type=jnp.float32)
    weighted = (weight_ref[0, 0] * filtered).astype(jnp.bfloat16).astype(jnp.float32)

    first_group = lax.broadcasted_iota(jnp.int32, (2 * share, LANES), 0) // share
    part = jnp.zeros((wafer_count * groups * share, LANES), jnp.float32)
    for k in range(Y):
        columns = []
        for n in range(chunks):
            for h in range(CHUNK // LANES):
                block = 2 * n + h
                at = n * rows + k // 2 * 2 * share
                both = weighted[at : at + 2 * share, h * LANES : (h + 1) * LANES]
                swapped = pltpu.roll(both, share, 0)
                mine = jnp.where(upper, both, swapped) if k % 2 == 0 else jnp.where(upper, swapped, both)
                group = (pix_all[k + 1, :, block * LANES : (block + 1) * LANES] >> 7) + (
                    groups * tile_all[k + 1, 0, block]
                )
                offset = group - first_group
                columns.append(
                    jnp.concatenate(
                        [jnp.where(offset == 2 * j, mine, 0.0) for j in range(wafer_count * groups // 2)],
                        axis=0,
                    ).astype(jnp.bfloat16)
                )
        part += lax.dot_general(
            jnp.concatenate(columns, axis=1),
            onehot_ref[k],
            (((1,), (1,)), ((), ())),
            preferred_element_type=jnp.float32,
        )
    for k in range(wafer_count):
        for j in range(groups):
            for sky in range(share):
                at, to = (k * groups + j) * share + sky, sky * groups + j
                part_ref[k, to // share, to % share : to % share + 1] = part[at : at + 1]

    copies = [send(part_ref.at[k], part_in.at[i], w_sem, i, d) for i, (k, d) in enumerate(zip(ws, w_ids))]
    wait_all(copies)
    total = part_ref[wafer]
    for i in range(wafer_count - 1):
        total += part_in[i]
    z_out[...] = total

    @pl.when(z < z_count - 1)
    def _():
        pl.semaphore_wait(z_ready, z_count - 1 - z)

    wait_all([send(z_out, z_in.at[i], z_sem, i, d) for i, d in enumerate(z_ids)])
    z_in[z_count - 1] = total
    total = jnp.zeros_like(total)
    for k in range(z_count):
        total += z_in[(z - k + z_count - 1) % z_count]
    sum_ref[...] = total

    copies = [send(sum_ref, out_ref.at[y], g_sem, i, d) for i, d in enumerate(y_ids)]
    own = pltpu.make_async_copy(sum_ref, out_ref.at[y], local_sem.at[1])
    own.start()
    own.wait()
    wait_all(copies)

    for copy in sends:
        copy.wait_send()

    @pl.when(gives_halo)
    def _():
        for copy in halo_tiles + halo_pixels:
            copy.wait_send()

    @pl.when(gives_taps)
    def _():
        for copy in tap_copies:
            copy.wait_send()


def solution(mesh):
    tm_count, wafer_count = mesh.shape["tm"], mesh.shape["wafer"]

    def per_device(sky, taps, weights, pixels, tiles):
        skies, _, pixel_count = sky.shape
        half, time_here, blocks = taps.shape[1], pixels.shape[1], tiles.shape[1]
        lead, chunks = 2 * half // CHUNK, time_here // CHUNK
        z_count, share = tm_count // Y, skies // Y
        hbm = pl.BlockSpec(memory_space=pltpu.HBM)
        f32, bf16, i32 = jnp.float32, jnp.bfloat16, jnp.int32
        piece = (pixel_count // LANES, share, LANES)
        sems = lambda n: pltpu.SemaphoreType.DMA((2, n))
        maps = pl.pallas_call(
            functools.partial(kernel, (tm_count, wafer_count)),
            out_shape=jax.ShapeDtypeStruct((Y,) + piece, f32),
            in_specs=[hbm] * 5,
            out_specs=hbm,
            scratch_shapes=[
                pltpu.VMEM((wafer_count, 16, pixel_count), bf16),
                pltpu.VMEM((wafer_count, 16 // share, share, pixel_count), f32),
                pltpu.VMEM((wafer_count, 2 * share, pixel_count), f32),
                pltpu.VMEM((2, 1, half), bf16),
                pltpu.SMEM((1, 1), f32),
                pltpu.VMEM((Y + 1, 1, time_here), i32),
                pltpu.VMEM((Y + 1, 1, blocks), i32),
                pltpu.SMEM((Y + 1, 1, blocks), i32),
                pltpu.VMEM((Y, LANES, time_here), bf16),
                pltpu.VMEM((LANES, 2 * half + 2 * CHUNK), bf16),
                pltpu.VMEM(((lead + chunks) * skies, CHUNK), bf16),
                pltpu.VMEM((wafer_count,) + piece, f32),
                pltpu.VMEM((wafer_count - 1,) + piece, f32),
                pltpu.VMEM(piece, f32),
                pltpu.VMEM((z_count,) + piece, f32),
                pltpu.VMEM(piece, f32),
                pltpu.SemaphoreType.DMA((5,)),
                sems(wafer_count - 1),
                sems(z_count),
                sems(2 * Y - 1),
                sems(2 * Y - 1),
                sems(wafer_count - 1),
                sems(z_count - 1),
                sems(Y - 1),
                pltpu.SemaphoreType.REGULAR,
                pltpu.SemaphoreType.REGULAR,
            ],
            compiler_params=pltpu.CompilerParams(
                collective_id=0, has_side_effects=True, vmem_limit_bytes=60 * 1024 * 1024
            ),
        )(sky.reshape(skies, pixel_count), taps, weights.reshape(1, 1), pixels, tiles)
        return maps.reshape(skies, 1, pixel_count)

    placed = (
        P("sim", "wafer", None),
        P("wafer", "sim"),
        P("wafer"),
        P("wafer", "tm"),
        P("wafer", "tm"),
    )
    return jax.shard_map(
        per_device, mesh=mesh, in_specs=placed, out_specs=P("sim", "wafer", None), check_vma=False
    )
```
